256 devices in a mesh: node: 32 (over z, y_hi, core), local: 8 (over y_lo, x).
Axes of the slice: x: 4, y: 4 (y_hi: 2, y_lo: 2; y = y_hi * 2 + y_lo), z: 8, core: 2. Of those that a mesh axis runs over, the one named last changes fastest.
Arguments:
- out_grad: bfloat16 [15360, 4096], P('node', 'local'), may hold values from -0.375 to 0.375
- gate_pre: bfloat16 [15360, 14336], P('node', 'local'), may hold values from -8 to 8
- up_pre: bfloat16 [15360, 14336], P('node', 'local'), may hold values from -6 to 6
- down_tiles: bfloat16 [4096, 14336], P('node', 'local'), may hold values from -4 to 4
- down_scales: float32 [32, 112], P('node', 'local'), may hold values from 0.19364917 to 1.9364917
Outputs:
- gate_grad: bfloat16 [15360, 14336], P('node', 'local')
- up_grad: bfloat16 [15360, 14336], P('node', 'local')
- down_grad: float32 [4096, 14336], P('node', 'local')
The draws below stay inside these ranges and needn't reach their ends.
All inputs are finite; a program needn't handle non-finite values.
Results may differ from the reference program's by a relative error of at most 0.019.
Values may be sent and summed in bfloat16 or wider, within the bound.
No kernel may reach another device: no remote copies, remote signals or barrier semaphores. Data moves between devices by JAX's collectives and lax.ppermute only.
A program may use at most 128 MiB of HBM per device.

```python
import math
import jax
import jax.numpy as jnp
from jax import lax

D = 4096
FF = 14336
BLK = 128
TOK_DEV = 480
TOKENS = 15360
N_NODE = 32


def raised(entries, stream_key, source, target, parts, factor):
    owner, partner = [(jnp.arange(entries.shape[axis_at]) // (entries.shape[axis_at] // parts)).reshape([-1 if axis == axis_at else 1 for axis in range(entries.ndim)]) for axis_at in (source, target)]
    chosen = jax.random.permutation(stream_key, parts)[partner]
    strong = (owner == chosen) | (owner == (partner + parts // 2) % parts)
    return jnp.where(strong, factor * entries, entries)


def block_levels(key, extent, split, least, top_value):
    factor_of = 1.0
    for position, parts in split:
        draws = jax.random.uniform(jax.random.fold_in(jax.random.fold_in(key, 6), position), (parts,), jnp.float32, least / len(split), top_value / len(split))
        factor_of = factor_of * jnp.repeat(jnp.exp(draws), extent[position] // parts).reshape((-1,) + (1,) * (len(extent) - 1 - position))
    return factor_of


def noise(key, shape, scale, limit, cuts=(), kind=jnp.bfloat16):
    drawn = scale * jax.random.normal(key, shape, jnp.float32)
    if cuts:
        drawn = drawn * block_levels(key, shape, cuts, -0.22, 0.18)
    return jnp.clip(drawn, -limit, limit).astype(kind)


def noise_with(rng, shape, deviation, most, split, heavy, held_as=jnp.bfloat16):
    drawn = deviation * jax.random.normal(rng, shape, jnp.float32)
    if split:
        drawn = drawn * block_levels(rng, shape, split, -0.22, 0.18)
    return jnp.clip(raised(drawn, jax.random.fold_in(rng, 3), *heavy), -most, most).astype(held_as)


def setup_inputs(seed: int = 0) -> dict:
    keys = jax.random.split(jax.random.key(seed), 6)
    out_grad = noise_with(keys[0], (TOKENS, D), (4.0 / (TOK_DEV * N_NODE) ** 0.5), 0.375, ((0, 32), (1, 8)), (0, 1, 32, 2.75))
    gate_pre = noise(keys[1], (TOKENS, FF), 1.5, 8.0, ((0, 32), (1, 8)))
    up_pre = noise(keys[2], (TOKENS, FF), 1.0, 6.0, ((0, 32), (1, 8)))
    down_tiles = noise(keys[3], (D, FF), 1.0, 4.0, ((0, 32), (1, 8)))
    down_scales = jnp.clip(jnp.exp(math.log(1.9364917) - 2.3025851 * jax.random.uniform(keys[4], (D // BLK, FF // BLK), jnp.float32) ** block_levels(keys[4], (D // BLK, FF // BLK), ((0, 32), (1, 8)), -0.2, 0.2)), 0.19364917, 1.9364917)
    return dict(out_grad=out_grad, gate_pre=gate_pre, up_pre=up_pre, down_tiles=down_tiles, down_scales=down_scales)


def dequantize(tiles, scales):
    rows, cols = tiles.shape
    side = rows // scales.shape[0]
    blocks = tiles.astype(jnp.float32).reshape(rows // side, side, cols // side, side)
    return (blocks * scales[:, None, :, None]).reshape(rows, cols).astype(jnp.bfloat16)


def reference(out_grad, gate_pre, up_pre, down_tiles, down_scales):
    weight = dequantize(down_tiles, down_scales)
    gate = gate_pre.astype(jnp.float32)
    up = up_pre.astype(jnp.float32)
    sig = jax.nn.sigmoid(gate)
    swish = gate * sig
    hidden = (swish * up).astype(jnp.bfloat16)
    hidden_grad = jnp.dot(out_grad, weight, preferred_element_type=jnp.float32)
    gate_grad = (hidden_grad * up * sig * (1.0 + gate * (1.0 - sig))).astype(jnp.bfloat16)
    up_grad = (hidden_grad * swish).astype(jnp.bfloat16)

    def node_term(carry, index):
        start = (index * TOK_DEV).astype(jnp.int32)
        grad_rows = lax.dynamic_slice_in_dim(out_grad, start, TOK_DEV, 0)
        hidden_rows = lax.dynamic_slice_in_dim(hidden, start, TOK_DEV, 0)
        term = lax.dot_general(grad_rows, hidden_rows, (((0,), (0,)), ((), ())), preferred_element_type=jnp.float32)
        rounded = lax.optimization_barrier(term.astype(jnp.bfloat16))
        return carry + rounded.astype(jnp.float32), None

    start_sum = jnp.zeros((D, FF), jnp.float32)
    down_grad, unused = lax.scan(node_term, start_sum, jnp.arange(N_NODE, dtype=jnp.int32))
    return gate_grad, up_grad, down_grad
```

```python
import jax
import jax.numpy as jnp
from jax import lax
from jax.experimental import pallas as pl
from jax.experimental.pallas import tpu as pltpu
from jax.sharding import Mesh, PartitionSpec as P

AXES = ("z", "yh", "c", "yl", "x")
SIZES = (8, 2, 2, 2, 4)
BF = jnp.bfloat16
F32 = jnp.float32
TOK = 480
SIDE = 128
TILE = 256
EARLY = 256
FIRST, REST = 1024, 768
SWAP = [(0, 1), (1, 0)]
PARAMS = pltpu.CompilerParams(vmem_limit_bytes=60 * 1024 * 1024)
ANY = pl.BlockSpec(memory_space=pl.ANY)
TOKEN = pl.BlockSpec(memory_space=pltpu.SMEM)
TOKEN_TYPE = jax.ShapeDtypeStruct((8,), jnp.int32)


def cost(flops, size):
    return pl.CostEstimate(flops=flops, bytes_accessed=size, transcendentals=0)


def dequantize(tiles, scales):
    rows, cols = tiles.shape
    side = rows // scales.shape[0]
    blocks = tiles.astype(F32).reshape(rows // side, side, cols // side, side)
    return (blocks * scales[:, None, :, None]).reshape(rows, cols).astype(BF)


def shift(value, axis, size, by):
    return lax.ppermute(value, axis, [(i, (i + by) % size) for i in range(size)])


def pass_token(places, order):
    for i in range(8):
        order[i] = places[i]


def down_kernel(places, *refs):
    grads, early, late = refs[:8], refs[8:12], refs[12:16]
    out, order, raw, turned, tall, ready, loaded, arrived, left = refs[16:]
    loads = [pltpu.make_async_copy(grads[i], raw.at[i], loaded.at[i]) for i in range(8)]
    cols = tall.shape[1]
    wide = [
        pltpu.make_async_copy(
            part[r], tall.at[pl.ds(r * TOK, TOK), pl.ds(at, size)], arrived.at[k, r]
        )
        for k, (part, at, size) in enumerate(((early, 0, EARLY), (late, EARLY, cols - EARLY)))
        for r in range(4)
    ]
    for copy in loads + wide:
        copy.start()
    for i in range(8):
        loads[i].wait()
        at = pl.multiple_of(places[i] * SIDE, SIDE)
        turned[pl.ds(at, SIDE), :] = raw[i].T
    pass_token(places, order)
    for copy in wide:
        copy.wait()
    stores = []
    for n in range(cols // TILE):
        at = pl.ds(n * TILE, TILE)
        ready[:, at] = jnp.dot(turned[...], tall[:, at], preferred_element_type=F32).astype(BF)
        stores.append(pltpu.make_async_copy(ready.at[:, at], out.at[:, at], left.at[n]))
        stores[n].start()
    for copy in stores:
        copy.wait()


def down_partial(places, grads, early, late):
    cols = early[0].shape[1] + late[0].shape[1]
    return pl.pallas_call(
        down_kernel,
        out_shape=(jax.ShapeDtypeStruct((8 * SIDE, cols), BF), TOKEN_TYPE),
        in_specs=[TOKEN] + [ANY] * 16,
        out_specs=(ANY, TOKEN),
        scratch_shapes=[
            pltpu.VMEM((8, 4 * TOK, SIDE), BF),
            pltpu.VMEM((8 * SIDE, 4 * TOK), BF),
            pltpu.VMEM((4 * TOK, cols), BF),
            pltpu.VMEM((8 * SIDE, cols), BF),
            pltpu.SemaphoreType.DMA((8,)),
            pltpu.SemaphoreType.DMA((2, 4)),
            pltpu.SemaphoreType.DMA((cols // TILE,)),
        ],
        compiler_params=PARAMS,
        cost_estimate=cost(2 * 8 * SIDE * 4 * TOK * cols, 14 << 20),
        name="down_partial",
    )(places, *grads, *early, *late)


def up_kernel(places, *refs):
    grads, weights, send, keep, pass_on, order, joined, sems = refs[:8], *refs[8:]

    @pl.when(pl.program_id(0) == 0)
    def _():
        loads = []
        for i in range(8):
            at = pl.ds(pl.multiple_of(places[i] * SIDE, SIDE), SIDE)
            loads.append(pltpu.make_async_copy(grads[i], joined.at[:, at], sems.at[i]))
            loads[i].start()
        pass_token(places, order)
        for copy in loads:
            copy.wait()

    w = weights[...]
    for r in range(4):
        rows = joined[r * TOK : (r + 1) * TOK, :]
        part = jnp.dot(rows, w, preferred_element_type=F32)
        if r % 2:
            send[r // 2] = part.astype(BF)
        elif r == 0:
            keep[...] = part
        else:
            pass_on[...] = part


def hidden_partial(places, grads, weights, start, cols):
    first = start // TILE
    one = pl.BlockSpec((TOK, TILE), lambda n: (0, n))
    return pl.pallas_call(
        up_kernel,
        out_shape=(
            jax.ShapeDtypeStruct((2, TOK, cols), BF),
            jax.ShapeDtypeStruct((TOK, cols), F32),
            jax.ShapeDtypeStruct((TOK, cols), F32),
            TOKEN_TYPE,
        ),
        grid=(cols // TILE,),
        in_specs=[TOKEN]
        + [ANY] * 8
        + [pl.BlockSpec((8 * SIDE, TILE), lambda n: (0, n + first))],
        out_specs=(pl.BlockSpec((2, TOK, TILE), lambda n: (0, 0, n)), one, one, TOKEN),
        scratch_shapes=[
            pltpu.VMEM((4 * TOK, 8 * SIDE), BF),
            pltpu.SemaphoreType.DMA((8,)),
        ],
        compiler_params=PARAMS,
        cost_estimate=cost(2 * 8 * SIDE * 4 * TOK * cols, 10 << 20),
        name="hidden_partial",
    )(places, *grads, weights)


def add_kernel(places, own, came, out, order):
    out[...] = (own[...] + came[...].astype(F32)).astype(BF)
    pass_token(places, order)


def add_partner(places, own, came):
    cols = own.shape[1]
    one = pl.BlockSpec((TOK, cols), lambda n: (0, 0))
    return pl.pallas_call(
        add_kernel,
        out_shape=(jax.ShapeDtypeStruct((TOK, cols), BF), TOKEN_TYPE),
        grid=(1,),
        in_specs=[TOKEN, one, pl.BlockSpec((None, TOK, cols), lambda n: (1, 0, 0))],
        out_specs=(one, TOKEN),
        compiler_params=PARAMS,
        cost_estimate=cost(TOK * cols, 8 * TOK * cols),
        name="add_partner",
    )(places, own, came)


def finish_kernel(gate_pre, up_pre, keep, came, far, *refs):
    gate_out, up_out = refs[-2:]
    hidden_grad = keep[...] + came[...].astype(F32) + far[...].astype(F32)
    gate = gate_pre[...].astype(F32)
    up = up_pre[...].astype(F32)
    sig = 0.5 + 0.5 * jnp.tanh(0.5 * gate)
    swish = gate * sig
    gate_out[...] = (hidden_grad * up * (sig + swish * (1.0 - sig))).astype(BF)
    up_out[...] = (hidden_grad * swish).astype(BF)


def finish(gate_pre, up_pre, keep, came, far, start, cols, made):
    first = start // TILE
    wide = pl.BlockSpec((TOK, TILE), lambda n: (0, n + first))
    one = pl.BlockSpec((TOK, TILE), lambda n: (0, n))
    half = pl.BlockSpec((None, TOK, TILE), lambda n: (0, 0, n))
    return pl.pallas_call(
        finish_kernel,
        out_shape=(jax.ShapeDtypeStruct(gate_pre.shape, BF),) * 2,
        grid=(cols // TILE,),
        in_specs=[wide, wide, one, half, one] + [ANY] * len(made),
        out_specs=(wide, wide),
        input_output_aliases={5 + i: i for i in range(len(made))},
        compiler_params=PARAMS,
        cost_estimate=cost(20 * TOK * cols, 16 * TOK * cols),
        name="finish",
    )(gate_pre, up_pre, keep, came, far, *made)


def per_device(out_grad, gate_pre, up_pre, down_tiles, down_scales):
    yh, c = lax.axis_index("yh"), lax.axis_index("c")
    yl, x = lax.axis_index("yl"), lax.axis_index("x")

    def block(r):
        other = 2 * (yh ^ (r >> 1)) + (c ^ (r & 1))
        return lax.dynamic_slice(out_grad, (0, other * SIDE), (TOK, SIDE))

    gate = gate_pre.astype(F32)
    h0 = (gate * jax.nn.sigmoid(gate) * up_pre.astype(F32)).astype(BF)
    ha, hb = h0[:, :EARLY], h0[:, EARLY:]
    near, ha = lax.optimization_barrier((lax.ppermute(block(1), "c", SWAP), ha))
    pieces = (
        block(0),
        near,
        lax.ppermute(block(2), "yh", SWAP),
        lax.ppermute(block(3), ("yh", "c"), [(i, 3 - i) for i in range(4)]),
    )
    ha2 = lax.ppermute(ha, "yh", SWAP)
    ha1 = lax.ppermute(ha, "c", SWAP)
    *pieces, ha1 = lax.optimization_barrier((*pieces, ha1))
    g = jnp.concatenate(pieces, axis=0)

    weight = dequantize(down_tiles, down_scales)
    weights = lax.all_gather(weight, "z", axis=0, tiled=True)

    gy = lax.ppermute(g, "yl", SWAP)
    g_m, g_p = shift(g, "x", 4, 1), shift(g, "x", 4, -1)
    gy, g_m, g_p, hb, ha2 = lax.optimization_barrier((gy, g_m, g_p, hb, ha2))
    gy_m, gy_p = shift(gy, "x", 4, 1), shift(gy, "x", 4, -1)
    g_far = shift(g_m, "x", 4, 1)
    hb2 = lax.ppermute(hb, "yh", SWAP)
    hb1, ha3 = lax.ppermute(hb, "c", SWAP), lax.ppermute(ha2, "c", SWAP)
    gy_far = shift(gy_p, "x", 4, -1)
    hb2, gy_m, g_far, gy_far, ha3, hb1 = lax.optimization_barrier(
        (hb2, gy_m, g_far, gy_far, ha3, hb1)
    )
    hb3 = lax.ppermute(hb2, "c", SWAP)

    grads = (g, gy, g_m, g_p, gy_m, gy_p, g_far, gy_far)
    places = jnp.stack(
        [
            (yl ^ dy) * 4 + ((x + dx) & 3)
            for dy, dx in ((0, 0), (1, 0), (0, 3), (0, 1), (1, 3), (1, 1), (0, 2), (1, 2))
        ]
    ).astype(jnp.int32)

    down, places = down_partial(places, grads, (ha, ha1, ha2, ha3), (hb, hb1, hb2, hb3))
    total = lax.psum_scatter(down, "z", scatter_dimension=0, tiled=True).astype(F32)

    send, keep_a, pass_on, places = hidden_partial(places, grads, weights, 0, FIRST)
    came_a = lax.ppermute(send, "c", SWAP)
    chip, places = add_partner(places, pass_on, came_a)
    far_a = lax.ppermute(chip, "yh", SWAP)

    send, keep_b, pass_on, places = hidden_partial(places, grads, weights, FIRST, REST)
    came_b = lax.ppermute(send, "c", SWAP)
    chip, places = add_partner(places, pass_on, came_b)
    far_b = lax.ppermute(chip, "yh", SWAP)

    made = finish(gate_pre, up_pre, keep_a, came_a, far_a, 0, FIRST, ())
    made = finish(gate_pre, up_pre, keep_b, came_b, far_b, FIRST, REST, made)
    return (*made, total)


def solution(mesh):
    fine = Mesh(mesh.devices.reshape(SIZES), AXES)
    spec = P(("z", "yh", "c"), ("yl", "x"))
    return jax.shard_map(
        per_device,
        mesh=fine,
        in_specs=(spec,) * 5,
        out_specs=(spec,) * 3,
        check_vma=False,
    )
```

```python
import functools

import jax
import jax.numpy as jnp
from jax import lax
from jax.experimental import pallas as pl
from jax.experimental.pallas import tpu as pltpu
from jax.sharding import Mesh, PartitionSpec as P

AXES = ("z", "yh", "c", "yl", "x")
SIZES = (8, 2, 2, 2, 4)
BF = jnp.bfloat16
F32 = jnp.float32
TOK = 480
SIDE = 128
TILE = 256
PARTS = (0, 512, 1024, 1792)
CUTS = (0, 768, 1536, 1792)
SWAP = [(0, 1), (1, 0)]
PARAMS = pltpu.CompilerParams(vmem_limit_bytes=60 * 1024 * 1024)
ANY = pl.BlockSpec(memory_space=pl.ANY)
TOKEN = pl.BlockSpec(memory_space=pltpu.SMEM)
TOKEN_TYPE = jax.ShapeDtypeStruct((8,), jnp.int32)


def cost(flops, size):
    return pl.CostEstimate(flops=flops, bytes_accessed=size, transcendentals=0)


def dequantize(tiles, scales):
    rows, cols = tiles.shape
    side = rows // scales.shape[0]
    blocks = tiles.astype(F32).reshape(rows // side, side, cols // side, side)
    return (blocks * scales[:, None, :, None]).reshape(rows, cols).astype(BF)


def shift(value, axis, size, by):
    return lax.ppermute(value, axis, [(i, (i + by) % size) for i in range(size)])


def pass_token(places, order):
    for i in range(8):
        order[i] = places[i]


def down_kernel(places, *refs):
    rows, hidden = refs[0], refs[1:13]
    out, order, turned, tall, ready, loaded, arrived, left = refs[13:]
    load = pltpu.make_async_copy(rows, turned, loaded)
    parts = [
        [
            pltpu.make_async_copy(
                hidden[4 * k + r],
                tall.at[pl.ds(r * TOK, TOK), pl.ds(PARTS[k], PARTS[k + 1] - PARTS[k])],
                arrived.at[k, r],
            )
            for r in range(4)
        ]
        for k in range(3)
    ]
    for copy in [load] + parts[0]:
        copy.start()
    pass_token(places, order)
    load.wait()
    for copy in parts[0]:
        copy.wait()
    for copy in parts[1] + parts[2]:
        copy.start()
    stores = []
    for n in range(tall.shape[1] // TILE):
        if n * TILE in PARTS[1:]:
            for copy in parts[PARTS.index(n * TILE)]:
                copy.wait()
        at = pl.ds(n * TILE, TILE)
        ready[:, at] = jnp.dot(turned[...], tall[:, at], preferred_element_type=F32).astype(BF)
        stores.append(pltpu.make_async_copy(ready.at[:, at], out.at[:, at], left.at[n]))
        stores[n].start()
    for copy in stores:
        copy.wait()


def down_partial(places, turned, hidden):
    cols = PARTS[-1]
    return pl.pallas_call(
        down_kernel,
        out_shape=(jax.ShapeDtypeStruct((8 * SIDE, cols), BF), TOKEN_TYPE),
        in_specs=[TOKEN] + [ANY] * 13,
        out_specs=(ANY, TOKEN),
        scratch_shapes=[
            pltpu.VMEM((8 * SIDE, 4 * TOK), BF),
            pltpu.VMEM((4 * TOK, cols), BF),
            pltpu.VMEM((8 * SIDE, cols), BF),
            pltpu.SemaphoreType.DMA,
            pltpu.SemaphoreType.DMA((3, 4)),
            pltpu.SemaphoreType.DMA((cols // TILE,)),
        ],
        compiler_params=PARAMS,
        cost_estimate=cost(1000, 1000),
        name="down_partial",
    )(places, turned, *hidden)


def up_kernel(spans, places, mine, their_own, their_far, weights, partner_weights, *refs):
    order, keep, *pass_on, joined, stacked, sems = refs
    n = pl.program_id(0)

    @pl.when(n == 0)
    def _():
        half = pl.ds(8 * SIDE, 8 * SIDE)
        targets = (
            joined.at[:, pl.ds(0, 8 * SIDE)],
            joined.at[pl.ds(0, TOK), half],
            joined.at[pl.ds(TOK, TOK), half],
        )
        loads = [
            pltpu.make_async_copy(source, target, sems.at[k])
            for k, (source, target) in enumerate(zip((mine, their_own, their_far), targets))
        ]
        for copy in loads:
            copy.start()
        pass_token(places, order)
        for copy in loads:
            copy.wait()

    stacked[: 8 * SIDE, :] = weights[...]
    stacked[8 * SIDE :, :] = partner_weights[...]
    part = jnp.dot(joined[...], stacked[...], preferred_element_type=F32)
    keep[...] = part[:TOK]
    other = part[TOK:].astype(BF)
    for (low, high), out in zip(spans, pass_on):

        @pl.when((n >= low) & (n < high))
        def _():
            out[...] = other


def hidden_partial(places, mine, theirs, weights, partner_weights, cuts):
    first, cols = cuts[0] // TILE, cuts[-1] - cuts[0]
    tiles = [(cut - cuts[0]) // TILE for cut in cuts]
    one = pl.BlockSpec((TOK, TILE), lambda n: (0, n))
    tile = pl.BlockSpec((8 * SIDE, TILE), lambda n: (0, n + first))

    def part(low, high):
        return pl.BlockSpec((TOK, TILE), lambda n: (0, jnp.clip(n - low, 0, high - low - 1)))

    spans = list(zip(tiles, tiles[1:]))
    return pl.pallas_call(
        functools.partial(up_kernel, spans),
        out_shape=(
            TOKEN_TYPE,
            jax.ShapeDtypeStruct((TOK, cols), F32),
            *(jax.ShapeDtypeStruct((TOK, (high - low) * TILE), BF) for low, high in spans),
        ),
        grid=(cols // TILE,),
        in_specs=[TOKEN, ANY, ANY, ANY, tile, tile],
        out_specs=(TOKEN, one, *(part(low, high) for low, high in spans)),
        scratch_shapes=[
            pltpu.VMEM((2 * TOK, 16 * SIDE), BF),
            pltpu.VMEM((16 * SIDE, TILE), BF),
            pltpu.SemaphoreType.DMA((3,)),
        ],
        compiler_params=PARAMS,
        cost_estimate=cost(1000, 1000),
        name="hidden_partial",
    )(places, mine, *theirs, weights, partner_weights)


def turn_kernel(places, *refs):
    grads, (turned, mine, send, send_far) = refs[:8], refs[8:]
    for i in range(8):
        at = pl.ds(pl.multiple_of(places[i] * SIDE, SIDE), SIDE)
        value = grads[i][...]
        turned[at, :] = value.T
        mine[:, at] = value[: 2 * TOK]
        send[:, at] = value[2 * TOK : 3 * TOK]
        send_far[:, at] = value[3 * TOK :]


def turn(places, grads):
    whole = pl.BlockSpec(memory_space=pltpu.VMEM)
    return pl.pallas_call(
        turn_kernel,
        out_shape=(
            jax.ShapeDtypeStruct((8 * SIDE, 4 * TOK), BF),
            jax.ShapeDtypeStruct((2 * TOK, 8 * SIDE), BF),
            jax.ShapeDtypeStruct((TOK, 8 * SIDE), BF),
            jax.ShapeDtypeStruct((TOK, 8 * SIDE), BF),
        ),
        in_specs=[TOKEN] + [whole] * 8,
        out_specs=(whole,) * 4,
        compiler_params=PARAMS,
        cost_estimate=cost(1000, 1000),
        name="turn",
    )(places, *grads)


def finish_kernel(gate_pre, up_pre, keep, far, *refs):
    gate_out, up_out = refs[-2:]
    hidden_grad = keep[...] + far[...].astype(F32)
    gate = gate_pre[...].astype(F32)
    up = up_pre[...].astype(F32)
    sig = 0.5 + 0.5 * jnp.tanh(0.5 * gate)
    swish = gate * sig
    gate_out[...] = (hidden_grad * up * (sig + swish * (1.0 - sig))).astype(BF)
    up_out[...] = (hidden_grad * swish).astype(BF)


def finish(gate_pre, up_pre, keep, far, start, keep_start, made):
    cols = far.shape[1]
    first, skip = start // TILE, keep_start // TILE
    wide = pl.BlockSpec((TOK, TILE), lambda n: (0, n + first))
    one = pl.BlockSpec((TOK, TILE), lambda n: (0, n))
    return pl.pallas_call(
        finish_kernel,
        out_shape=(jax.ShapeDtypeStruct(gate_pre.shape, BF),) * 2,
        grid=(cols // TILE,),
        in_specs=[wide, wide, pl.BlockSpec((TOK, TILE), lambda n: (0, n + skip)), one] + [ANY] * len(made),
        out_specs=(wide, wide),
        input_output_aliases={4 + i: i for i in range(len(made))},
        compiler_params=PARAMS,
        cost_estimate=cost(20 * TOK * cols, 16 * TOK * cols),
        name="finish",
    )(gate_pre, up_pre, keep, far, *made)


def per_device(out_grad, gate_pre, up_pre, down_tiles, down_scales):
    yh, c = lax.axis_index("yh"), lax.axis_index("c")
    yl, x = lax.axis_index("yl"), lax.axis_index("x")

    def block(r):
        other = 2 * (yh ^ (r >> 1)) + (c ^ (r & 1))
        return lax.dynamic_slice(out_grad, (0, other * SIDE), (TOK, SIDE))

    gate = gate_pre.astype(F32)
    h0 = (gate * jax.nn.sigmoid(gate) * up_pre.astype(F32)).astype(BF)
    hb, hc, hd = (h0[:, PARTS[k] : PARTS[k + 1]] for k in range(3))
    blocks = [block(r) for r in range(4)]
    down_tiles, *blocks = lax.optimization_barrier((down_tiles, *blocks))
    pieces = [
        blocks[0],
        lax.ppermute(blocks[2], "yh", SWAP),
        lax.ppermute(blocks[1], "c", SWAP),
        lax.ppermute(blocks[3], ("yh", "c"), [(i, 3 - i) for i in range(4)]),
    ]
    g = jnp.concatenate(pieces, axis=0)

    weight = dequantize(down_tiles, down_scales)
    weights = lax.all_gather(weight, "z", axis=0, tiled=True)

    gy = lax.ppermute(g, "yl", SWAP)
    g_m, g_p = shift(g, "x", 4, 1), shift(g, "x", 4, -1)
    hb1, hc1, hd1 = (lax.ppermute(h, "c", SWAP) for h in (hb, hc, hd))
    gy, g_m, g_p, hb, hb1 = lax.optimization_barrier((gy, g_m, g_p, hb, hb1))
    gy_m, gy_p = shift(gy, "x", 4, 1), shift(gy, "x", 4, -1)
    hb2 = lax.ppermute(hb, "yh", SWAP)
    hc, hb2, gy_m, gy_p, g_m, hc1 = lax.optimization_barrier((hc, hb2, gy_m, gy_p, g_m, hc1))
    hc2 = lax.ppermute(hc, "yh", SWAP)
    g_far, gy_far = shift(g_m, "x", 4, 1), shift(gy_p, "x", 4, -1)
    hb3 = lax.ppermute(hb2, "c", SWAP)
    g_far, gy_far, weights, hb3, hc2, hd, hd1 = lax.optimization_barrier(
        (g_far, gy_far, weights, hb3, hc2, hd, hd1)
    )
    hd2 = lax.ppermute(hd, "yh", SWAP)
    hc3 = lax.ppermute(hc2, "c", SWAP)
    partner_weights = lax.ppermute(weights, "c", SWAP)
    places = jnp.stack(
        [
            (yl ^ dy) * 4 + ((x + dx) & 3)
            for dy, dx in ((0, 0), (1, 0), (0, 3), (0, 1), (1, 3), (1, 1), (0, 2), (1, 2))
        ]
    ).astype(jnp.int32)
    turned, mine, *send = turn(places, (g, gy, g_m, g_p, gy_m, gy_p, g_far, gy_far))
    theirs = [lax.ppermute(v, "c", SWAP) for v in send]
    hd3 = lax.ppermute(hd2, "c", SWAP)
    partner_weights, turned, theirs, hc3, hd3 = lax.optimization_barrier(
        (partner_weights, turned, theirs, hc3, hd3)
    )
    hidden = (hb, hb2, hb1, hb3, hc, hc2, hc1, hc3, hd, hd2, hd1, hd3)
    down, places = down_partial(places, turned, hidden)
    total = lax.psum_scatter(down, "z", scatter_dimension=0, tiled=True).astype(F32)

    made, found = (), []
    for cuts in (CUTS[:2], CUTS[1:]):
        places, keep, *passed = hidden_partial(
            places, mine, theirs, weights, partner_weights, cuts
        )
        for start, value in zip(cuts, passed):
            far = lax.ppermute(value, "yh", SWAP)
            found.append((keep, far, start, start - cuts[0]))
    for keep, far, start, inside in found:
        made = finish(gate_pre, up_pre, keep, far, start, inside, made)
    return (*made, total)


def solution(mesh):
    fine = Mesh(mesh.devices.reshape(SIZES), AXES)
    spec = P(("z", "yh", "c"), ("yl", "x"))
    return jax.shard_map(
        per_device,
        mesh=fine,
        in_specs=(spec,) * 5,
        out_specs=(spec,) * 3,
        check_vma=False,
    )
```

```python
import functools

import jax
import jax.numpy as jnp
from jax import lax
from jax.experimental import pallas as pl
from jax.experimental.pallas import tpu as pltpu
from jax.sharding import Mesh, PartitionSpec as P

AXES = ("z", "yh", "c", "yl", "x")
SIZES = (8, 2, 2, 2, 4)
BF = jnp.bfloat16
F32 = jnp.float32
TOK = 480
SIDE = 128
TILE = 256
PARTS = (0, 512, 1024, 1792)
CUTS = (0, 512, 1024, 1536, 1792)
SWAP = [(0, 1), (1, 0)]
PARAMS = pltpu.CompilerParams(vmem_limit_bytes=60 * 1024 * 1024)
ANY = pl.BlockSpec(memory_space=pl.ANY)
TOKEN = pl.BlockSpec(memory_space=pltpu.SMEM)
TOKEN_TYPE = jax.ShapeDtypeStruct((8,), jnp.int32)


def cost(flops, size):
    return pl.CostEstimate(flops=flops, bytes_accessed=size, transcendentals=0)


def dequantize(tiles, scales):
    rows, cols = tiles.shape
    side = rows // scales.shape[0]
    blocks = tiles.astype(F32).reshape(rows // side, side, cols // side, side)
    return (blocks * scales[:, None, :, None]).reshape(rows, cols).astype(BF)


def shift(value, axis, size, by):
    return lax.ppermute(value, axis, [(i, (i + by) % size) for i in range(size)])


def pass_token(places, order):
    for i in range(8):
        order[i] = places[i]


def down_kernel(places, *refs):
    rows, hidden = refs[0], refs[1:13]
    out, order, turned, tall, ready, loaded, arrived, left = refs[13:]
    load = pltpu.make_async_copy(rows, turned, loaded)
    parts = [
        [
            pltpu.make_async_copy(
                hidden[4 * k + r],
                tall.at[pl.ds(r * TOK, TOK), pl.ds(PARTS[k], PARTS[k + 1] - PARTS[k])],
                arrived.at[k, r],
            )
            for r in range(4)
        ]
        for k in range(3)
    ]
    for copy in [load] + parts[0]:
        copy.start()
    pass_token(places, order)
    load.wait()
    for copy in parts[0]:
        copy.wait()
    for copy in parts[1] + parts[2]:
        copy.start()
    stores = []
    for n in range(tall.shape[1] // TILE):
        if n * TILE in PARTS[1:]:
            for copy in parts[PARTS.index(n * TILE)]:
                copy.wait()
        at = pl.ds(n * TILE, TILE)
        ready[:, at] = jnp.dot(turned[...], tall[:, at], preferred_element_type=F32).astype(BF)
        stores.append(pltpu.make_async_copy(ready.at[:, at], out.at[:, at], left.at[n]))
        stores[n].start()
    for copy in stores:
        copy.wait()


def down_partial(places, turned, hidden):
    cols = PARTS[-1]
    return pl.pallas_call(
        down_kernel,
        out_shape=(jax.ShapeDtypeStruct((8 * SIDE, cols), BF), TOKEN_TYPE),
        in_specs=[TOKEN] + [ANY] * 13,
        out_specs=(ANY, TOKEN),
        scratch_shapes=[
            pltpu.VMEM((8 * SIDE, 4 * TOK), BF),
            pltpu.VMEM((4 * TOK, cols), BF),
            pltpu.VMEM((8 * SIDE, cols), BF),
            pltpu.SemaphoreType.DMA,
            pltpu.SemaphoreType.DMA((3, 4)),
            pltpu.SemaphoreType.DMA((cols // TILE,)),
        ],
        compiler_params=PARAMS,
        cost_estimate=cost(1000, 1000),
        name="down_partial",
    )(places, turned, *hidden)


def up_kernel(spans, places, mine, their_own, their_far, weights, partner_weights, *refs):
    order, keep, *pass_on, joined, stacked, sems = refs
    n = pl.program_id(0)

    @pl.when(n == 0)
    def _():
        half = pl.ds(8 * SIDE, 8 * SIDE)
        targets = (
            joined.at[:, pl.ds(0, 8 * SIDE)],
            joined.at[pl.ds(0, TOK), half],
            joined.at[pl.ds(TOK, TOK), half],
        )
        loads = [
            pltpu.make_async_copy(source, target, sems.at[k])
            for k, (source, target) in enumerate(zip((mine, their_own, their_far), targets))
        ]
        for copy in loads:
            copy.start()
        pass_token(places, order)
        for copy in loads:
            copy.wait()

    stacked[: 8 * SIDE, :] = weights[...]
    stacked[8 * SIDE :, :] = partner_weights[...]
    part = jnp.dot(joined[...], stacked[...], preferred_element_type=F32)
    keep[...] = part[:TOK]
    other = part[TOK:].astype(BF)
    for (low, high), out in zip(spans, pass_on):

        @pl.when((n >= low) & (n < high))
        def _():
            out[...] = other


def hidden_partial(places, mine, theirs, weights, partner_weights, cuts):
    first, cols = cuts[0] // TILE, cuts[-1] - cuts[0]
    tiles = [(cut - cuts[0]) // TILE for cut in cuts]
    one = pl.BlockSpec((TOK, TILE), lambda n: (0, n))
    tile = pl.BlockSpec((8 * SIDE, TILE), lambda n: (0, n + first))

    def part(low, high):
        return pl.BlockSpec((TOK, TILE), lambda n: (0, jnp.clip(n - low, 0, high - low - 1)))

    spans = list(zip(tiles, tiles[1:]))
    return pl.pallas_call(
        functools.partial(up_kernel, spans),
        out_shape=(
            TOKEN_TYPE,
            jax.ShapeDtypeStruct((TOK, cols), F32),
            *(jax.ShapeDtypeStruct((TOK, (high - low) * TILE), BF) for low, high in spans),
        ),
        grid=(cols // TILE,),
        in_specs=[TOKEN, ANY, ANY, ANY, tile, tile],
        out_specs=(TOKEN, one, *(part(low, high) for low, high in spans)),
        scratch_shapes=[
            pltpu.VMEM((2 * TOK, 16 * SIDE), BF),
            pltpu.VMEM((16 * SIDE, TILE), BF),
            pltpu.SemaphoreType.DMA((3,)),
        ],
        compiler_params=PARAMS,
        cost_estimate=cost(1000, 1000),
        name="hidden_partial",
    )(places, mine, *theirs, weights, partner_weights)


def turn_kernel(places, *refs):
    grads, (turned, mine, send, send_far) = refs[:8], refs[8:]
    for i in range(8):
        at = pl.ds(pl.multiple_of(places[i] * SIDE, SIDE), SIDE)
        value = grads[i][...]
        turned[at, :] = value.T
        mine[:, at] = value[: 2 * TOK]
        send[:, at] = value[2 * TOK : 3 * TOK]
        send_far[:, at] = value[3 * TOK :]


def turn(places, grads):
    whole = pl.BlockSpec(memory_space=pltpu.VMEM)
    return pl.pallas_call(
        turn_kernel,
        out_shape=(
            jax.ShapeDtypeStruct((8 * SIDE, 4 * TOK), BF),
            jax.ShapeDtypeStruct((2 * TOK, 8 * SIDE), BF),
            jax.ShapeDtypeStruct((TOK, 8 * SIDE), BF),
            jax.ShapeDtypeStruct((TOK, 8 * SIDE), BF),
        ),
        in_specs=[TOKEN] + [whole] * 8,
        out_specs=(whole,) * 4,
        compiler_params=PARAMS,
        cost_estimate=cost(1000, 1000),
        name="turn",
    )(places, *grads)


def finish_kernel(last, gate_pre, up_pre, keep, far, *refs):
    gate_out, up_out = refs[-3:-1] if last else refs[-2:]
    if last:
        refs[-1][...] = refs[0][...].astype(F32)
    hidden_grad = keep[...] + far[...].astype(F32)
    gate = gate_pre[...].astype(F32)
    up = up_pre[...].astype(F32)
    sig = 0.5 + 0.5 * jnp.tanh(0.5 * gate)
    swish = gate * sig
    gate_out[...] = (hidden_grad * up * (sig + swish * (1.0 - sig))).astype(BF)
    up_out[...] = (hidden_grad * swish).astype(BF)


def finish(gate_pre, up_pre, keep, far, start, keep_start, made, last=()):
    cols = far.shape[1]
    first, skip = start // TILE, keep_start // TILE
    wide = pl.BlockSpec((TOK, TILE), lambda n: (0, n + first))
    one = pl.BlockSpec((TOK, TILE), lambda n: (0, n))
    kept = pl.BlockSpec((TOK, TILE), lambda n: (0, n + skip))
    whole = [pl.BlockSpec(v.shape, lambda n: (0, 0)) for v in last]
    return pl.pallas_call(
        functools.partial(finish_kernel, len(last)),
        out_shape=(
            *(jax.ShapeDtypeStruct(gate_pre.shape, BF),) * 2,
            *(jax.ShapeDtypeStruct(v.shape, F32) for v in last),
        ),
        grid=(cols // TILE,),
        in_specs=[wide, wide, kept, one] + whole + [ANY] * len(made),
        out_specs=(wide, wide, *whole),
        input_output_aliases={4 + len(last) + i: i for i in range(len(made))},
        compiler_params=PARAMS,
        cost_estimate=cost(20 * TOK * cols, 16 * TOK * cols),
        name="finish",
    )(gate_pre, up_pre, keep, far, *last, *made)


def per_device(out_grad, gate_pre, up_pre, down_tiles, down_scales):
    yh, c = lax.axis_index("yh"), lax.axis_index("c")
    yl, x = lax.axis_index("yl"), lax.axis_index("x")

    def block(r):
        other = 2 * (yh ^ (r >> 1)) + (c ^ (r & 1))
        return lax.dynamic_slice(out_grad, (0, other * SIDE), (TOK, SIDE))

    gate = gate_pre.astype(F32)
    h0 = (gate * jax.nn.sigmoid(gate) * up_pre.astype(F32)).astype(BF)
    hb, hc, hd = (h0[:, PARTS[k] : PARTS[k + 1]] for k in range(3))
    blocks = [block(r) for r in range(4)]
    down_tiles, *blocks = lax.optimization_barrier((down_tiles, *blocks))
    pieces = [
        blocks[0],
        lax.ppermute(blocks[2], "yh", SWAP),
        lax.ppermute(blocks[1], "c", SWAP),
        lax.ppermute(blocks[3], ("yh", "c"), [(i, 3 - i) for i in range(4)]),
    ]
    g = jnp.concatenate(pieces, axis=0)

    weight = dequantize(down_tiles, down_scales)
    weights = lax.all_gather(weight, "z", axis=0, tiled=True)

    gy = lax.ppermute(g, "yl", SWAP)
    g_m, g_p = shift(g, "x", 4, 1), shift(g, "x", 4, -1)
    hb1, hc1, hd1 = (lax.ppermute(h, "c", SWAP) for h in (hb, hc, hd))
    gy, g_m, g_p, hb, hb1 = lax.optimization_barrier((gy, g_m, g_p, hb, hb1))
    gy_m, gy_p = shift(gy, "x", 4, 1), shift(gy, "x", 4, -1)
    hb2 = lax.ppermute(hb, "yh", SWAP)
    hc, hb2, hc1 = lax.optimization_barrier((hc, hb2, hc1))
    g_m, gy_m = lax.optimization_barrier((g_m, gy_m))
    hc2 = lax.ppermute(hc, "yh", SWAP)
    g_far, gy_far = shift(g_m, "x", 4, 1), shift(gy_p, "x", 4, -1)
    hb3 = lax.ppermute(hb2, "c", SWAP)
    g_far, gy_far, weights, hb3, hc2, hd, hd1 = lax.optimization_barrier(
        (g_far, gy_far, weights, hb3, hc2, hd, hd1)
    )
    hd2 = lax.ppermute(hd, "yh", SWAP)
    hc3 = lax.ppermute(hc2, "c", SWAP)
    partner_weights = lax.ppermute(weights, "c", SWAP)
    places = jnp.stack(
        [
            (yl ^ dy) * 4 + ((x + dx) & 3)
            for dy, dx in ((0, 0), (1, 0), (0, 3), (0, 1), (1, 3), (1, 1), (0, 2), (1, 2))
        ]
    ).astype(jnp.int32)
    turned, mine, *send = turn(places, (g, gy, g_m, g_p, gy_m, gy_p, g_far, gy_far))
    theirs = [lax.ppermute(v, "c", SWAP) for v in send]
    hd3 = lax.ppermute(hd2, "c", SWAP)
    partner_weights, turned, theirs, hc3, hd3 = lax.optimization_barrier(
        (partner_weights, turned, theirs, hc3, hd3)
    )
    hidden = (hb, hb2, hb1, hb3, hc, hc2, hc1, hc3, hd, hd2, hd1, hd3)
    down, places = down_partial(places, turned, hidden)
    total = lax.psum_scatter(down, "z", scatter_dimension=0, tiled=True)

    made, found = (), []
    for cuts in (CUTS[:2], CUTS[1:]):
        places, keep, *passed = hidden_partial(
            places, mine, theirs, weights, partner_weights, cuts
        )
        for start, value in zip(cuts, passed):
            far = lax.ppermute(value, "yh", SWAP)
            found.append((keep, far, start, start - cuts[0]))
    for keep, far, start, inside in found:
        last = (total,) if start == CUTS[-2] else ()
        made = finish(gate_pre, up_pre, keep, far, start, inside, made, last)
    return made


def solution(mesh):
    fine = Mesh(mesh.devices.reshape(SIZES), AXES)
    spec = P(("z", "yh", "c"), ("yl", "x"))
    return jax.shard_map(
        per_device,
        mesh=fine,
        in_specs=(spec,) * 5,
        out_specs=(spec,) * 3,
        check_vma=False,
    )
```

```python
import functools

import jax
import jax.numpy as jnp
from jax import lax
from jax.experimental import pallas as pl
from jax.experimental.pallas import tpu as pltpu
from jax.sharding import Mesh, PartitionSpec as P

AXES = ("z", "yh", "c", "yl", "x")
SIZES = (8, 2, 2, 2, 4)
BF = jnp.bfloat16
F32 = jnp.float32
TOK = 480
SIDE = 128
TILE = 256
PARTS = (0, 512, 1024, 1792)
CUTS = (0, 512, 1024, 1536, 1792)
SWAP = [(0, 1), (1, 0)]
PARAMS = pltpu.CompilerParams(vmem_limit_bytes=60 * 1024 * 1024)
ANY = pl.BlockSpec(memory_space=pl.ANY)
TOKEN = pl.BlockSpec(memory_space=pltpu.SMEM)
TOKEN_TYPE = jax.ShapeDtypeStruct((8,), jnp.int32)


def cost(flops, size):
    return pl.CostEstimate(flops=flops, bytes_accessed=size, transcendentals=0)


def dequantize(tiles, scales):
    rows, cols = tiles.shape
    side = rows // scales.shape[0]
    blocks = tiles.astype(F32).reshape(rows // side, side, cols // side, side)
    return (blocks * scales[:, None, :, None]).reshape(rows, cols).astype(BF)


def shift(value, axis, size, by):
    return lax.ppermute(value, axis, [(i, (i + by) % size) for i in range(size)])


def pass_token(places, order):
    for i in range(8):
        order[i] = places[i]


def down_kernel(bounds, places, *refs):
    count = len(bounds) - 1
    rows, hidden = refs[0], refs[1 : 1 + 4 * count]
    out, order, turned, tall, ready, loaded, arrived, left = refs[-8:]
    base = bounds[0]
    load = pltpu.make_async_copy(rows, turned, loaded)
    parts = [
        pltpu.make_async_copy(
            hidden[4 * k + r],
            tall.at[pl.ds(r * TOK, TOK), pl.ds(bounds[k] - base, bounds[k + 1] - bounds[k])],
            arrived.at[k, r],
        )
        for k in range(count)
        for r in range(4)
    ]
    for copy in [load] + parts:
        copy.start()
    pass_token(places, order)
    for copy in [load] + parts:
        copy.wait()
    stores = []
    for n in range(tall.shape[1] // TILE):
        at = pl.ds(n * TILE, TILE)
        ready[:, at] = jnp.dot(turned[...], tall[:, at], preferred_element_type=F32).astype(BF)
        to = out.at[:, pl.ds(base + n * TILE, TILE)]
        stores.append(pltpu.make_async_copy(ready.at[:, at], to, left.at[n]))
        stores[n].start()
    for copy in stores:
        copy.wait()


def down_partial(places, turned, hidden, bounds, made=()):
    cols, count = bounds[-1] - bounds[0], len(bounds) - 1
    return pl.pallas_call(
        functools.partial(down_kernel, bounds),
        out_shape=(jax.ShapeDtypeStruct((8 * SIDE, PARTS[-1]), BF), TOKEN_TYPE),
        in_specs=[TOKEN] + [ANY] * (1 + 4 * count + len(made)),
        out_specs=(ANY, TOKEN),
        input_output_aliases={2 + 4 * count: 0} if made else {},
        scratch_shapes=[
            pltpu.VMEM((8 * SIDE, 4 * TOK), BF),
            pltpu.VMEM((4 * TOK, cols), BF),
            pltpu.VMEM((8 * SIDE, cols), BF),
            pltpu.SemaphoreType.DMA,
            pltpu.SemaphoreType.DMA((count, 4)),
            pltpu.SemaphoreType.DMA((cols // TILE,)),
        ],
        compiler_params=PARAMS,
        cost_estimate=cost(1000, 1000),
        name="down_partial",
    )(places, turned, *hidden, *made)


def up_kernel(spans, places, mine, their_own, their_far, weights, partner_weights, *refs):
    order, keep, *pass_on, joined, stacked, sems = refs
    n = pl.program_id(0)

    @pl.when(n == 0)
    def _():
        half = pl.ds(8 * SIDE, 8 * SIDE)
        targets = (
            joined.at[:, pl.ds(0, 8 * SIDE)],
            joined.at[pl.ds(0, TOK), half],
            joined.at[pl.ds(TOK, TOK), half],
        )
        loads = [
            pltpu.make_async_copy(source, target, sems.at[k])
            for k, (source, target) in enumerate(zip((mine, their_own, their_far), targets))
        ]
        for copy in loads:
            copy.start()
        pass_token(places, order)
        for copy in loads:
            copy.wait()

    stacked[: 8 * SIDE, :] = weights[...]
    stacked[8 * SIDE :, :] = partner_weights[...]
    part = jnp.dot(joined[...], stacked[...], preferred_element_type=F32)
    keep[...] = part[:TOK]
    other = part[TOK:].astype(BF)
    for (low, high), out in zip(spans, pass_on):

        @pl.when((n >= low) & (n < high))
        def _():
            out[...] = other


def hidden_partial(places, mine, theirs, weights, partner_weights, cuts):
    first, cols = cuts[0] // TILE, cuts[-1] - cuts[0]
    tiles = [(cut - cuts[0]) // TILE for cut in cuts]
    one = pl.BlockSpec((TOK, TILE), lambda n: (0, n))
    tile = pl.BlockSpec((8 * SIDE, TILE), lambda n: (0, n + first))

    def part(low, high):
        return pl.BlockSpec((TOK, TILE), lambda n: (0, jnp.clip(n - low, 0, high - low - 1)))

    spans = list(zip(tiles, tiles[1:]))
    return pl.pallas_call(
        functools.partial(up_kernel, spans),
        out_shape=(
            TOKEN_TYPE,
            jax.ShapeDtypeStruct((TOK, cols), F32),
            *(jax.ShapeDtypeStruct((TOK, (high - low) * TILE), BF) for low, high in spans),
        ),
        grid=(cols // TILE,),
        in_specs=[TOKEN, ANY, ANY, ANY, tile, tile],
        out_specs=(TOKEN, one, *(part(low, high) for low, high in spans)),
        scratch_shapes=[
            pltpu.VMEM((2 * TOK, 16 * SIDE), BF),
            pltpu.VMEM((16 * SIDE, TILE), BF),
            pltpu.SemaphoreType.DMA((3,)),
        ],
        compiler_params=PARAMS,
        cost_estimate=cost(1000, 1000),
        name="hidden_partial",
    )(places, mine, *theirs, weights, partner_weights)


def turn_kernel(places, *refs):
    grads, (turned, mine, send, send_far) = refs[:8], refs[8:]
    for i in range(8):
        at = pl.ds(pl.multiple_of(places[i] * SIDE, SIDE), SIDE)
        value = grads[i][...]
        turned[at, :] = value.T
        mine[:, at] = value[: 2 * TOK]
        send[:, at] = value[2 * TOK : 3 * TOK]
        send_far[:, at] = value[3 * TOK :]


def turn(places, grads):
    whole = pl.BlockSpec(memory_space=pltpu.VMEM)
    return pl.pallas_call(
        turn_kernel,
        out_shape=(
            jax.ShapeDtypeStruct((8 * SIDE, 4 * TOK), BF),
            jax.ShapeDtypeStruct((2 * TOK, 8 * SIDE), BF),
            jax.ShapeDtypeStruct((TOK, 8 * SIDE), BF),
            jax.ShapeDtypeStruct((TOK, 8 * SIDE), BF),
        ),
        in_specs=[TOKEN] + [whole] * 8,
        out_specs=(whole,) * 4,
        compiler_params=PARAMS,
        cost_estimate=cost(1000, 1000),
        name="turn",
    )(places, *grads)


def finish_kernel(last, gate_pre, up_pre, keep, far, *refs):
    gate_out, up_out = refs[-3:-1] if last else refs[-2:]
    if last:
        refs[-1][...] = refs[0][...].astype(F32)
    hidden_grad = keep[...] + far[...].astype(F32)
    gate = gate_pre[...].astype(F32)
    up = up_pre[...].astype(F32)
    sig = 0.5 + 0.5 * jnp.tanh(0.5 * gate)
    swish = gate * sig
    gate_out[...] = (hidden_grad * up * (sig + swish * (1.0 - sig))).astype(BF)
    up_out[...] = (hidden_grad * swish).astype(BF)


def finish(gate_pre, up_pre, keep, far, start, keep_start, made, last=()):
    cols = far.shape[1]
    first, skip = start // TILE, keep_start // TILE
    wide = pl.BlockSpec((TOK, TILE), lambda n: (0, n + first))
    one = pl.BlockSpec((TOK, TILE), lambda n: (0, n))
    kept = pl.BlockSpec((TOK, TILE), lambda n: (0, n + skip))
    whole = [pl.BlockSpec(v.shape, lambda n: (0, 0)) for v in last]
    return pl.pallas_call(
        functools.partial(finish_kernel, len(last)),
        out_shape=(
            *(jax.ShapeDtypeStruct(gate_pre.shape, BF),) * 2,
            *(jax.ShapeDtypeStruct(v.shape, F32) for v in last),
        ),
        grid=(cols // TILE,),
        in_specs=[wide, wide, kept, one] + whole + [ANY] * len(made),
        out_specs=(wide, wide, *whole),
        input_output_aliases={4 + len(last) + i: i for i in range(len(made))},
        compiler_params=PARAMS,
        cost_estimate=cost(20 * TOK * cols, 16 * TOK * cols),
        name="finish",
    )(gate_pre, up_pre, keep, far, *last, *made)


def per_device(out_grad, gate_pre, up_pre, down_tiles, down_scales):
    yh, c = lax.axis_index("yh"), lax.axis_index("c")
    yl, x = lax.axis_index("yl"), lax.axis_index("x")

    def block(r):
        other = 2 * (yh ^ (r >> 1)) + (c ^ (r & 1))
        return lax.dynamic_slice(out_grad, (0, other * SIDE), (TOK, SIDE))

    gate = gate_pre.astype(F32)
    h0 = (gate * jax.nn.sigmoid(gate) * up_pre.astype(F32)).astype(BF)
    hb, hc, hd = (h0[:, PARTS[k] : PARTS[k + 1]] for k in range(3))
    blocks = [block(r) for r in range(4)]
    down_tiles, *blocks = lax.optimization_barrier((down_tiles, *blocks))
    pieces = [
        blocks[0],
        lax.ppermute(blocks[2], "yh", SWAP),
        lax.ppermute(blocks[1], "c", SWAP),
        lax.ppermute(blocks[3], ("yh", "c"), [(i, 3 - i) for i in range(4)]),
    ]
    g = jnp.concatenate(pieces, axis=0)

    weight = dequantize(down_tiles, down_scales)
    weights = lax.all_gather(weight, "z", axis=0, tiled=True)

    gy = lax.ppermute(g, "yl", SWAP)
    g_m, g_p = shift(g, "x", 4, 1), shift(g, "x", 4, -1)
    hb1, hc1, hd1 = (lax.ppermute(h, "c", SWAP) for h in (hb, hc, hd))
    gy, g_m, g_p, hb, hb1 = lax.optimization_barrier((gy, g_m, g_p, hb, hb1))
    gy_m, gy_p = shift(gy, "x", 4, 1), shift(gy, "x", 4, -1)
    hb2 = lax.ppermute(hb, "yh", SWAP)
    hc, hb2, hc1 = lax.optimization_barrier((hc, hb2, hc1))
    g_m, gy_m = lax.optimization_barrier((g_m, gy_m))
    hc2 = lax.ppermute(hc, "yh", SWAP)
    g_far, gy_far = shift(g_m, "x", 4, 1), shift(gy_p, "x", 4, -1)
    hb3 = lax.ppermute(hb2, "c", SWAP)
    g_far, gy_far, weights, hb3, hc2, hd, hd1 = lax.optimization_barrier(
        (g_far, gy_far, weights, hb3, hc2, hd, hd1)
    )
    hd2 = lax.ppermute(hd, "yh", SWAP)
    hc3 = lax.ppermute(hc2, "c", SWAP)
    partner_weights = lax.ppermute(weights, "c", SWAP)
    places = jnp.stack(
        [
            (yl ^ dy) * 4 + ((x + dx) & 3)
            for dy, dx in ((0, 0), (1, 0), (0, 3), (0, 1), (1, 3), (1, 1), (0, 2), (1, 2))
        ]
    ).astype(jnp.int32)
    turned, mine, *send = turn(places, (g, gy, g_m, g_p, gy_m, gy_p, g_far, gy_far))
    hidden = (hb, hb2, hb1, hb3, hc, hc2, hc1, hc3)
    down, places = down_partial(places, turned, hidden, PARTS[:3])
    down, *send = lax.optimization_barrier((down, *send))
    theirs = [lax.ppermute(v, "c", SWAP) for v in send]
    hd3 = lax.ppermute(hd2, "c", SWAP)
    partner_weights, turned, theirs, down, hd3 = lax.optimization_barrier(
        (partner_weights, turned, theirs, down, hd3)
    )
    down, places = down_partial(places, turned, (hd, hd2, hd1, hd3), PARTS[2:], (down,))
    total = lax.psum_scatter(down, "z", scatter_dimension=0, tiled=True)

    made, found = (), []
    for cuts in (CUTS[:2], CUTS[1:]):
        places, keep, *passed = hidden_partial(
            places, mine, theirs, weights, partner_weights, cuts
        )
        for start, value in zip(cuts, passed):
            far = lax.ppermute(value, "yh", SWAP)
            found.append((keep, far, start, start - cuts[0]))
    for keep, far, start, inside in found:
        last = (total,) if start == CUTS[-2] else ()
        made = finish(gate_pre, up_pre, keep, far, start, inside, made, last)
    return made


def solution(mesh):
    fine = Mesh(mesh.devices.reshape(SIZES), AXES)
    spec = P(("z", "yh", "c"), ("yl", "x"))
    return jax.shard_map(
        per_device,
        mesh=fine,
        in_specs=(spec,) * 5,
        out_specs=(spec,) * 3,
        check_vma=False,
    )
```
